32 devices in a mesh: row: 4 (over y, x), col: 8 (over z, core).
Axes of the slice: x: 2, y: 2, z: 4, core: 2. Of those that a mesh axis runs over, the one named last changes fastest.
Arguments:
- source_amps: float32 [1024, 6144], P(('row', 'col')), may hold values from -6 to 6
- row_owner: int32 [4, 256], replicated, may hold values from 0 to 255, each once within a row
- integrals: float32 [6144, 2048], P('row', 'col'), may hold values from -0.078125 to 0.078125
- occ_energy: float32 [1024], P('row'), may hold values from -2 to -0.5
- vir_energy: float32 [2048], P('col'), may hold values from 0.5 to 3
Outputs:
- increment: float32 [1024, 2048], P('row', 'col')
The draws below stay inside these ranges and needn't reach their ends.
Inputs may be any that keep to these rules, and one draw needn't show every extreme that they name: Each row of row_owner holds every number below 256 once.
All inputs are finite; a program needn't handle non-finite values.
Results may differ from the reference program's by a relative error of at most 0.00007.
Values sent between devices are 32-bit elements; how exact they have to be, the bound alone decides.
A program may use at most 64 MiB of HBM per device.

```python
import jax
import jax.numpy as jnp
from jax import lax

MROW = 256
K = 6144
M = 1024
N = 2048
N_ROW = 4


def block_scale(rng, shape, split, smallest, top_value):
    level = 1.0
    for dim, parts in split:
        draws = jax.random.uniform(jax.random.fold_in(jax.random.fold_in(rng, 6), dim), (parts,), jnp.float32, smallest / len(split), top_value / len(split))
        level = level * jnp.repeat(jnp.exp(draws), shape[dim] // parts).reshape((-1,) + (1,) * (len(shape) - 1 - dim))
    return level


def gaussian(stream_key, dims, scale, bound, pieces=(), dtype=jnp.bfloat16):
    drawn = scale * jax.random.normal(stream_key, dims, jnp.float32)
    if pieces:
        drawn = drawn * block_scale(stream_key, dims, pieces, -0.22, 0.18)
    return jnp.clip(drawn, -bound, bound).astype(dtype)


def setup_inputs(seed: int = 0) -> dict:
    splits = jax.random.split(jax.random.key(seed), 6)
    return {
        "source_amps": gaussian(splits[0], (M, K), 1.0, 6.0, ((0, 32),), jnp.float32),
        "row_owner": jax.vmap(lambda own: jax.random.permutation(own, MROW))(jax.random.split(splits[1], N_ROW)).reshape((N_ROW, MROW)).astype(jnp.int32),
        "integrals": gaussian(splits[2], (K, N), K ** -0.5, 0.078125, ((0, 4), (1, 8)), jnp.float32),
        "occ_energy": jnp.clip(-2.0 + 1.5 * jax.random.uniform(splits[3], (M,), jnp.float32) ** block_scale(splits[3], (M,), ((0, 4),), -0.2, 0.2), -2.0, -0.5),
        "vir_energy": jnp.clip(0.5 + 2.5 * jax.random.uniform(splits[4], (N,), jnp.float32) ** block_scale(splits[4], (N,), ((0, 8),), -0.2, 0.2), 0.5, 3.0),
    }


def place_rows(block_rows, owners):
    return jnp.zeros_like(block_rows).at[owners].set(block_rows)


def reference(source_amps, row_owner, integrals, occ_energy, vir_energy):
    groups = source_amps.reshape(N_ROW, MROW, K)
    placed = jax.vmap(place_rows)(groups, row_owner)
    amplitudes = placed.reshape(N_ROW * MROW, K)
    ladder = jnp.dot(amplitudes, integrals, precision=lax.Precision.HIGHEST, preferred_element_type=jnp.float32)
    return ladder / (vir_energy[None, :] - occ_energy[:, None])
```

```python
import functools

import jax
import jax.numpy as jnp
from jax import lax
from jax.experimental import pallas as pl
from jax.experimental.pallas import tpu as pltpu
from jax.sharding import PartitionSpec as P

MESH = pl.DeviceIdType.MESH
TAIL_PART = (0, 12)


def split2(x):
    hi = x.astype(jnp.bfloat16)
    return hi, (x - hi.astype(jnp.float32)).astype(jnp.bfloat16)


def dot(a, b):
    return jnp.dot(a, b, preferred_element_type=jnp.float32)


def flip(r, j, n):
    out, bit = 0, 1
    while bit < n:
        rb, jb = (r // bit) % 2, (j // bit) % 2
        out = out + bit * (rb + jb - 2 * rb * jb)
        bit *= 2
    return out


def kernel(
    R, Z, F,
    amps, owner, integrals, occ, vir, out,
    a_all, b_raw, b_hi, b_lo, part, slots, ladder, off_raw, off_hi, off_lo, off_part, off_slots, off_sum,
    own_recv, mate_recv, slot_recv, right_send, left_send, mate_send, slot_send, swap_send, load_sem,
    off_recv, off_send, sum_send, b_send, b_recv,
):
    r = lax.axis_index("row")
    c = lax.axis_index("col")
    z, co = c // 2, c % 2
    D = amps.shape[0]
    Kr = integrals.shape[0]
    H = Kr - F
    E = Z * R
    rows = 2 * D
    lower = (z < Z // 2).astype(jnp.int32)
    way = 2 * lower - 1
    n_out = jnp.minimum(z, Z - 1 - z)
    at_end = n_out == 0
    beside_end = n_out == 1
    end_z = (1 - lower) * (Z - 1)

    def event(e):
        f = e - 2 * R
        g = f - 2 * R * n_out
        first = e < 2 * R
        paired = f < 2 * R * n_out
        dist = jnp.where(
            first, e // R,
            jnp.where(paired, jnp.where(f % 2 == 0, -(f // (2 * R) + 1), f // (2 * R) + 2), n_out + 2 + g // R),
        )
        j = jnp.where(first, e % R, jnp.where(paired, (f % (2 * R)) // 2, g % R))
        return z + way * dist, flip(r, j, R), dist, j

    def block_copy(zs, rs, width, z_to, c_to, send_sem, recv_sem):
        ref = a_all.at[zs, rs, co, :, pl.ds(0, width)]
        return pltpu.make_async_remote_copy(
            src_ref=ref, dst_ref=ref, send_sem=send_sem, recv_sem=recv_sem.at[zs, rs],
            device_id=(r, z_to * 2 + c_to), device_id_type=MESH,
        )

    def by_width(head_only, fn):
        if F == 0:
            fn(Kr)
            return

        @pl.when(head_only)
        def _():
            fn(H)

        @pl.when(jnp.logical_not(head_only))
        def _():
            fn(Kr)

    def forward(e, act):
        zs, rs, _, _ = event(e)

        def right(width):
            act(block_copy(zs, rs, width, z + 1, co, right_send.at[zs, rs], own_recv))

        def left(width):
            act(block_copy(zs, rs, width, z - 1, co, left_send.at[zs, rs], own_recv))

        def mate(width):
            act(block_copy(zs, rs, width, z, 1 - co, mate_send.at[zs, rs], mate_recv))

        @pl.when((zs <= z) & (z < Z - 1))
        def _():
            by_width(z + 1 == Z - 1, right)

        @pl.when((zs >= z) & (z > 0))
        def _():
            by_width(z - 1 == 0, left)

        by_width(at_end & (zs != z), mate)

    def await_block(e, sem, core):
        zs, rs, _, _ = event(e)

        def wait(width):
            ref = a_all.at[zs, rs, core, :, pl.ds(0, width)]
            pltpu.make_async_copy(ref, ref, sem.at[zs, rs]).wait()

        by_width(at_end & (zs != z), wait)

    def product(zs, rs, start, width, hi, lo):
        x = a_all[zs, rs, :, :, start:start + width].reshape(rows, width)
        x_hi, x_lo = split2(x)
        return dot(x_hi, hi) + (dot(x_lo, hi) + dot(x_hi, lo))

    def slot_copy(zs, rs):
        return pltpu.make_async_remote_copy(
            src_ref=part.at[zs, rs], dst_ref=slots.at[zs, r], send_sem=slot_send.at[zs, rs],
            recv_sem=slot_recv.at[zs, r], device_id=(rs, c), device_id_type=MESH,
        )

    def off_copy(zs, rs):
        return pltpu.make_async_remote_copy(
            src_ref=off_part.at[zs, rs], dst_ref=off_slots.at[zs, r], send_sem=off_send.at[zs, rs],
            recv_sem=off_recv.at[zs, r], device_id=(rs, c), device_id_type=MESH,
        )

    def sum_copy(zs):
        return pltpu.make_async_remote_copy(
            src_ref=off_sum.at[zs], dst_ref=slots.at[zs, R], send_sem=sum_send.at[zs],
            recv_sem=slot_recv.at[zs, R], device_id=(r, end_z * 2 + co), device_id_type=MESH,
        )

    def off_product(zs, rs):
        off_part[zs, rs] = product(zs, rs, H, F, off_hi[...], off_lo[...])

        @pl.when(rs != r)
        def _():
            off_copy(zs, rs).start()

    def compute(e):
        zs, rs, dist, j = event(e)
        await_block(e, mate_recv, 1 - co)

        def main(width):
            part[zs, rs] = product(zs, rs, 0, width, b_hi[0:width, :], b_lo[0:width, :])

        by_width(at_end & (zs != z), main)

        @pl.when(rs != r)
        def _():
            slot_copy(zs, rs).start()

        if F:
            @pl.when(beside_end & (dist == -1))
            def _():
                @pl.when(j == 0)
                def _():
                    pltpu.make_async_copy(off_raw, off_raw, b_recv).wait()
                    off_hi[...], off_lo[...] = split2(off_raw[...])

                off_product(z, rs)
                off_product(z + way, rs)

            @pl.when(beside_end & (dist >= 2))
            def _():
                off_product(zs, rs)

    def reduce_off(zs):
        total = off_part[zs, r]
        for k in range(1, R):
            other = flip(r, k, R)
            ref = off_slots.at[zs, other]
            pltpu.make_async_copy(ref, ref, off_recv.at[zs, other]).wait()
            total = total + off_slots[zs, other]
        off_sum[zs] = total
        sum_copy(zs).start()

    def b_tail_copy():
        return pltpu.make_async_remote_copy(
            src_ref=integrals.at[pl.ds(H, F), :], dst_ref=off_raw, send_sem=b_send, recv_sem=b_recv,
            device_id=(r, (end_z + way) * 2 + co), device_id_type=MESH,
        )

    def swap_copy(k):
        other = flip(r, k, R)
        return pltpu.make_async_remote_copy(
            src_ref=amps.at[:, pl.ds(pl.multiple_of(other * Kr, 128), Kr)], dst_ref=a_all.at[z, r, co],
            send_sem=swap_send.at[k], recv_sem=own_recv.at[z, r], device_id=(other, c), device_id_type=MESH,
        )

    mine = pltpu.make_async_copy(
        amps.at[:, pl.ds(pl.multiple_of(r * Kr, 128), Kr)], a_all.at[z, r, co], own_recv.at[z, r]
    )
    mine.start()
    load_b = pltpu.make_async_copy(integrals, b_raw, load_sem)
    load_b.start()

    barrier = pltpu.get_barrier_semaphore()

    def greet(device):
        pl.semaphore_signal(barrier, inc=1, device_id=device, device_id_type=MESH)

    for k in range(1, R):
        greet((flip(r, k, R), c))
    greet((r, z * 2 + 1 - co))

    @pl.when(z > 0)
    def _():
        greet((r, c - 2))

    @pl.when(z < Z - 1)
    def _():
        greet((r, c + 2))

    pl.semaphore_wait(barrier, R + (z > 0).astype(jnp.int32) + (z < Z - 1).astype(jnp.int32))

    for k in range(1, R):
        swap_copy(k).start()
    if F:
        @pl.when(at_end)
        def _():
            b_tail_copy().start()

    def start(copy):
        copy.start()

    await_block(0, own_recv, co)
    forward(0, start)
    load_b.wait()
    b_hi[...], b_lo[...] = split2(b_raw[...])

    @pl.loop(1, E)
    def _(e):
        await_block(e, own_recv, co)
        forward(e, start)
        compute(e - 1)

    if F:
        @pl.when(beside_end)
        def _():
            reduce_off(z)
            reduce_off(z + way)

    compute(E - 1)
    if F:
        @pl.when(beside_end)
        def _():
            for d in range(2, Z - 1):
                reduce_off(z + way * d)

    for zs in range(Z):
        total = part[zs, r]
        for k in range(1, R):
            other = flip(r, k, R)
            ref = slots.at[zs, other]
            pltpu.make_async_copy(ref, ref, slot_recv.at[zs, other]).wait()
            total = total + slots[zs, other]
        ladder[zs * rows:(zs + 1) * rows, :] = total
        if F:
            @pl.when(at_end & (z != zs))
            def _(zs=zs):
                ref = slots.at[zs, R]
                pltpu.make_async_copy(ref, ref, slot_recv.at[zs, R]).wait()
                ladder[zs * rows:(zs + 1) * rows, :] += slots[zs, R]

    G = out.shape[0]
    place = (lax.broadcasted_iota(jnp.int32, (G, G), 0) == owner[pl.ds(r, 1), :]).astype(jnp.float32).astype(jnp.bfloat16)
    x = ladder[...]
    h0 = x.astype(jnp.bfloat16)
    x = x - h0.astype(jnp.float32)
    h1, h2 = split2(x)
    placed = (dot(place, h2) + dot(place, h1)) + dot(place, h0)
    diagonal = lax.broadcasted_iota(jnp.int32, (G, G), 0) == lax.broadcasted_iota(jnp.int32, (G, G), 1)
    occ_column = jnp.sum(jnp.where(diagonal, occ[...], 0.0), axis=1, keepdims=True)
    out[...] = placed / (vir[...] - occ_column)

    def wait_send(copy):
        copy.wait_send()

    for k in range(1, R):
        swap_copy(k).wait_send()
    if F:
        @pl.when(at_end)
        def _():
            b_tail_copy().wait_send()

    @pl.loop(0, E)
    def _(e):
        zs, rs, dist, j = event(e)
        forward(e, wait_send)

        @pl.when(rs != r)
        def _():
            slot_copy(zs, rs).wait_send()

        if F:
            @pl.when(beside_end & (dist != -1))
            def _():
                @pl.when(rs != r)
                def _():
                    off_copy(zs, rs).wait_send()

                @pl.when(j == 0)
                def _():
                    sum_copy(zs).wait_send()


def solution(mesh):
    R, C = mesh.shape["row"], mesh.shape["col"]
    Z = C // 2

    def per_device(amps, row_owner, integrals, occ, vir):
        D = amps.shape[0]
        Kr, N = integrals.shape
        F = Kr * TAIL_PART[0] // TAIL_PART[1] // 128 * 128 if Z >= 4 else 0
        f = max(F, 128)
        G = occ.shape[0]
        rows = 2 * D
        f32, bf16 = jnp.float32, jnp.bfloat16
        dma = pltpu.SemaphoreType.DMA
        vmem = pl.BlockSpec(memory_space=pltpu.VMEM)
        hbm = pl.BlockSpec(memory_space=pl.ANY)
        return pl.pallas_call(
            functools.partial(kernel, R, Z, F),
            out_shape=jax.ShapeDtypeStruct((G, N), f32),
            in_specs=[hbm, vmem, hbm, vmem, vmem],
            out_specs=vmem,
            scratch_shapes=[
                pltpu.VMEM((Z, R, 2, D, Kr), f32),
                pltpu.VMEM((Kr, N), f32),
                pltpu.VMEM((Kr, N), bf16),
                pltpu.VMEM((Kr, N), bf16),
                pltpu.VMEM((Z, R, rows, N), f32),
                pltpu.VMEM((Z, R + 1, rows, N), f32),
                pltpu.VMEM((G, N), f32),
                pltpu.VMEM((f, N), f32),
                pltpu.VMEM((f, N), bf16),
                pltpu.VMEM((f, N), bf16),
                pltpu.VMEM((Z, R, rows, N), f32),
                pltpu.VMEM((Z, R, rows, N), f32),
                pltpu.VMEM((Z, rows, N), f32),
                dma((Z, R)), dma((Z, R)), dma((Z, R + 1)),
                dma((Z, R)), dma((Z, R)), dma((Z, R)), dma((Z, R)), dma((R,)), dma,
                dma((Z, R)), dma((Z, R)), dma((Z,)), dma, dma,
            ],
            compiler_params=pltpu.CompilerParams(
                collective_id=0, has_side_effects=True, vmem_limit_bytes=48 * 1024 * 1024
            ),
        )(amps, row_owner, integrals, occ.reshape(1, -1), vir.reshape(1, -1))

    return jax.shard_map(
        per_device,
        mesh=mesh,
        in_specs=(P(("row", "col"), None), P(), P("row", "col"), P("row"), P("col")),
        out_specs=P("row", "col"),
        check_vma=False,
    )
```

```python
import functools

import jax
import jax.numpy as jnp
from jax import lax
from jax.experimental import pallas as pl
from jax.experimental.pallas import tpu as pltpu
from jax.sharding import PartitionSpec as P

MESH = pl.DeviceIdType.MESH
TAIL_PART = (5, 12)


def split2(x):
    hi = x.astype(jnp.bfloat16)
    return hi, (x - hi.astype(jnp.float32)).astype(jnp.bfloat16)


def dot(a, b):
    return jnp.dot(a, b, preferred_element_type=jnp.float32)


def flip(r, j, n):
    out, bit = 0, 1
    while bit < n:
        rb, jb = (r // bit) % 2, (j // bit) % 2
        out = out + bit * (rb + jb - 2 * rb * jb)
        bit *= 2
    return out


def kernel(
    R, Z, F,
    amps, owner, integrals, occ, vir, out,
    a_all, b_raw, b_hi, b_lo, part, slots, ladder, off_raw, off_hi, off_lo, off_part, off_slots, off_sum,
    own_recv, mate_recv, slot_recv, right_send, left_send, mate_send, slot_send, swap_send, load_sem,
    off_recv, off_send, sum_send, b_send, b_recv,
):
    r = lax.axis_index("row")
    c = lax.axis_index("col")
    z, co = c // 2, c % 2
    D = amps.shape[0]
    Kr = integrals.shape[0]
    H = Kr - F
    E = Z * R
    rows = 2 * D
    lower = (z < Z // 2).astype(jnp.int32)
    way = 2 * lower - 1
    n_out = jnp.minimum(z, Z - 1 - z)
    at_end = n_out == 0
    beside_end = n_out == 1
    end_z = (1 - lower) * (Z - 1)

    def event(e):
        f = e - 2 * R
        g = f - 2 * R * n_out
        first = e < 2 * R
        paired = f < 2 * R * n_out
        dist = jnp.where(
            first, e // R,
            jnp.where(paired, jnp.where(f % 2 == 0, -(f // (2 * R) + 1), f // (2 * R) + 2), n_out + 2 + g // R),
        )
        j = jnp.where(first, e % R, jnp.where(paired, (f % (2 * R)) // 2, g % R))
        return z + way * dist, flip(r, j, R), dist, j

    def block_copy(zs, rs, width, z_to, c_to, send_sem, recv_sem):
        ref = a_all.at[zs, rs, co, :, pl.ds(0, width)]
        return pltpu.make_async_remote_copy(
            src_ref=ref, dst_ref=ref, send_sem=send_sem, recv_sem=recv_sem.at[zs, rs],
            device_id=(r, z_to * 2 + c_to), device_id_type=MESH,
        )

    def by_width(head_only, fn):
        if F == 0:
            fn(Kr)
            return

        @pl.when(head_only)
        def _():
            fn(H)

        @pl.when(jnp.logical_not(head_only))
        def _():
            fn(Kr)

    def forward(e, act):
        zs, rs, _, _ = event(e)

        def right(width):
            act(block_copy(zs, rs, width, z + 1, co, right_send.at[zs, rs], own_recv))

        def left(width):
            act(block_copy(zs, rs, width, z - 1, co, left_send.at[zs, rs], own_recv))

        def mate(width):
            act(block_copy(zs, rs, width, z, 1 - co, mate_send.at[zs, rs], mate_recv))

        @pl.when((zs <= z) & (z < Z - 1))
        def _():
            by_width(z + 1 == Z - 1, right)

        @pl.when((zs >= z) & (z > 0))
        def _():
            by_width(z - 1 == 0, left)

        by_width(at_end & (zs != z), mate)

    def await_block(e, sem, core):
        zs, rs, _, _ = event(e)

        def wait(width):
            ref = a_all.at[zs, rs, core, :, pl.ds(0, width)]
            pltpu.make_async_copy(ref, ref, sem.at[zs, rs]).wait()

        by_width(at_end & (zs != z), wait)

    def product(zs, rs, start, width, hi, lo):
        x = a_all[zs, rs, :, :, start:start + width].reshape(rows, width)
        x_hi, x_lo = split2(x)
        return dot(x_hi, hi) + (dot(x_lo, hi) + dot(x_hi, lo))

    def slot_copy(zs, rs):
        return pltpu.make_async_remote_copy(
            src_ref=part.at[zs, rs], dst_ref=slots.at[zs, r], send_sem=slot_send.at[zs, rs],
            recv_sem=slot_recv.at[zs, r], device_id=(rs, c), device_id_type=MESH,
        )

    def off_copy(zs, rs):
        return pltpu.make_async_remote_copy(
            src_ref=off_part.at[zs, rs], dst_ref=off_slots.at[zs, r], send_sem=off_send.at[zs, rs],
            recv_sem=off_recv.at[zs, r], device_id=(rs, c), device_id_type=MESH,
        )

    def sum_copy(zs):
        return pltpu.make_async_remote_copy(
            src_ref=off_sum.at[zs], dst_ref=slots.at[zs, R], send_sem=sum_send.at[zs],
            recv_sem=slot_recv.at[zs, R], device_id=(r, end_z * 2 + co), device_id_type=MESH,
        )

    def off_product(zs, rs):
        off_part[zs, rs] = product(zs, rs, H, F, off_hi[...], off_lo[...])

        @pl.when(rs != r)
        def _():
            off_copy(zs, rs).start()

    def compute(e):
        zs, rs, dist, j = event(e)
        await_block(e, mate_recv, 1 - co)

        def main(width):
            part[zs, rs] = product(zs, rs, 0, width, b_hi[0:width, :], b_lo[0:width, :])

        by_width(at_end & (zs != z), main)

        @pl.when(rs != r)
        def _():
            slot_copy(zs, rs).start()

        if F:
            @pl.when(beside_end & (dist == -1))
            def _():
                @pl.when(j == 0)
                def _():
                    pltpu.make_async_copy(off_raw, off_raw, b_recv).wait()
                    off_hi[...], off_lo[...] = split2(off_raw[...])

                off_product(z, rs)
                off_product(z + way, rs)

            @pl.when(beside_end & (dist >= 2))
            def _():
                off_product(zs, rs)

    def reduce_off(zs):
        total = off_part[zs, r]
        for k in range(1, R):
            other = flip(r, k, R)
            ref = off_slots.at[zs, other]
            pltpu.make_async_copy(ref, ref, off_recv.at[zs, other]).wait()
            total = total + off_slots[zs, other]
        off_sum[zs] = total
        sum_copy(zs).start()

    def b_tail_copy():
        return pltpu.make_async_remote_copy(
            src_ref=integrals.at[pl.ds(H, F), :], dst_ref=off_raw, send_sem=b_send, recv_sem=b_recv,
            device_id=(r, (end_z + way) * 2 + co), device_id_type=MESH,
        )

    def swap_copy(k):
        other = flip(r, k, R)
        return pltpu.make_async_remote_copy(
            src_ref=amps.at[:, pl.ds(pl.multiple_of(other * Kr, 128), Kr)], dst_ref=a_all.at[z, r, co],
            send_sem=swap_send.at[k], recv_sem=own_recv.at[z, r], device_id=(other, c), device_id_type=MESH,
        )

    mine = pltpu.make_async_copy(
        amps.at[:, pl.ds(pl.multiple_of(r * Kr, 128), Kr)], a_all.at[z, r, co], own_recv.at[z, r]
    )
    mine.start()
    load_b = pltpu.make_async_copy(integrals, b_raw, load_sem)
    load_b.start()

    barrier = pltpu.get_barrier_semaphore()

    def greet(device):
        pl.semaphore_signal(barrier, inc=1, device_id=device, device_id_type=MESH)

    for k in range(1, R):
        greet((flip(r, k, R), c))
    greet((r, z * 2 + 1 - co))

    @pl.when(z > 0)
    def _():
        greet((r, c - 2))

    @pl.when(z < Z - 1)
    def _():
        greet((r, c + 2))

    pl.semaphore_wait(barrier, R + (z > 0).astype(jnp.int32) + (z < Z - 1).astype(jnp.int32))

    for k in range(1, R):
        swap_copy(k).start()
    if F:
        @pl.when(at_end)
        def _():
            b_tail_copy().start()

    def start(copy):
        copy.start()

    await_block(0, own_recv, co)
    forward(0, start)
    load_b.wait()
    b_hi[...], b_lo[...] = split2(b_raw[...])

    @pl.loop(1, E)
    def _(e):
        await_block(e, own_recv, co)
        forward(e, start)
        compute(e - 1)

    if F:
        @pl.when(beside_end)
        def _():
            reduce_off(z)
            reduce_off(z + way)

    compute(E - 1)
    if F:
        @pl.when(beside_end)
        def _():
            for d in range(2, Z - 1):
                reduce_off(z + way * d)

    for zs in range(Z):
        total = part[zs, r]
        for k in range(1, R):
            other = flip(r, k, R)
            ref = slots.at[zs, other]
            pltpu.make_async_copy(ref, ref, slot_recv.at[zs, other]).wait()
            total = total + slots[zs, other]
        ladder[zs * rows:(zs + 1) * rows, :] = total
        if F:
            @pl.when(at_end & (z != zs))
            def _(zs=zs):
                ref = slots.at[zs, R]
                pltpu.make_async_copy(ref, ref, slot_recv.at[zs, R]).wait()
                ladder[zs * rows:(zs + 1) * rows, :] += slots[zs, R]

    G = out.shape[0]
    place = (lax.broadcasted_iota(jnp.int32, (G, G), 0) == owner[pl.ds(r, 1), :]).astype(jnp.float32).astype(jnp.bfloat16)
    x = ladder[...]
    h0 = x.astype(jnp.bfloat16)
    x = x - h0.astype(jnp.float32)
    h1, h2 = split2(x)
    placed = (dot(place, h2) + dot(place, h1)) + dot(place, h0)
    diagonal = lax.broadcasted_iota(jnp.int32, (G, G), 0) == lax.broadcasted_iota(jnp.int32, (G, G), 1)
    occ_column = jnp.sum(jnp.where(diagonal, occ[...], 0.0), axis=1, keepdims=True)
    out[...] = placed / (vir[...] - occ_column)

    def wait_send(copy):
        copy.wait_send()

    for k in range(1, R):
        swap_copy(k).wait_send()
    if F:
        @pl.when(at_end)
        def _():
            b_tail_copy().wait_send()

    @pl.loop(0, E)
    def _(e):
        zs, rs, dist, j = event(e)
        forward(e, wait_send)

        @pl.when(rs != r)
        def _():
            slot_copy(zs, rs).wait_send()

        if F:
            @pl.when(beside_end & (dist != -1))
            def _():
                @pl.when(rs != r)
                def _():
                    off_copy(zs, rs).wait_send()

                @pl.when(j == 0)
                def _():
                    sum_copy(zs).wait_send()


def solution(mesh):
    R, C = mesh.shape["row"], mesh.shape["col"]
    Z = C // 2

    def per_device(amps, row_owner, integrals, occ, vir):
        D = amps.shape[0]
        Kr, N = integrals.shape
        F = Kr * TAIL_PART[0] // TAIL_PART[1] // 128 * 128 if Z >= 4 else 0
        f = max(F, 128)
        G = occ.shape[0]
        rows = 2 * D
        f32, bf16 = jnp.float32, jnp.bfloat16
        dma = pltpu.SemaphoreType.DMA
        vmem = pl.BlockSpec(memory_space=pltpu.VMEM)
        hbm = pl.BlockSpec(memory_space=pl.ANY)
        return pl.pallas_call(
            functools.partial(kernel, R, Z, F),
            out_shape=jax.ShapeDtypeStruct((G, N), f32),
            in_specs=[hbm, vmem, hbm, vmem, vmem],
            out_specs=vmem,
            scratch_shapes=[
                pltpu.VMEM((Z, R, 2, D, Kr), f32),
                pltpu.VMEM((Kr, N), f32),
                pltpu.VMEM((Kr, N), bf16),
                pltpu.VMEM((Kr, N), bf16),
                pltpu.VMEM((Z, R, rows, N), f32),
                pltpu.VMEM((Z, R + 1, rows, N), f32),
                pltpu.VMEM((G, N), f32),
                pltpu.VMEM((f, N), f32),
                pltpu.VMEM((f, N), bf16),
                pltpu.VMEM((f, N), bf16),
                pltpu.VMEM((Z, R, rows, N), f32),
                pltpu.VMEM((Z, R, rows, N), f32),
                pltpu.VMEM((Z, rows, N), f32),
                dma((Z, R)), dma((Z, R)), dma((Z, R + 1)),
                dma((Z, R)), dma((Z, R)), dma((Z, R)), dma((Z, R)), dma((R,)), dma,
                dma((Z, R)), dma((Z, R)), dma((Z,)), dma, dma,
            ],
            compiler_params=pltpu.CompilerParams(
                collective_id=0, has_side_effects=True, vmem_limit_bytes=48 * 1024 * 1024
            ),
        )(amps, row_owner, integrals, occ.reshape(1, -1), vir.reshape(1, -1))

    return jax.shard_map(
        per_device,
        mesh=mesh,
        in_specs=(P(("row", "col"), None), P(), P("row", "col"), P("row"), P("col")),
        out_specs=P("row", "col"),
        check_vma=False,
    )
```

```python
import functools

import jax
import jax.numpy as jnp
from jax import lax
from jax.experimental import pallas as pl
from jax.experimental.pallas import tpu as pltpu
from jax.sharding import PartitionSpec as P

MESH = pl.DeviceIdType.MESH
TAIL_PART = (0, 12)


def split2(x):
    hi = x.astype(jnp.bfloat16)
    return hi, (x - hi.astype(jnp.float32)).astype(jnp.bfloat16)


def dot(a, b):
    return jnp.dot(a, b, preferred_element_type=jnp.float32)


def flip(r, j, n):
    out, bit = 0, 1
    while bit < n:
        rb, jb = (r // bit) % 2, (j // bit) % 2
        out = out + bit * (rb + jb - 2 * rb * jb)
        bit *= 2
    return out


def kernel(
    R, Z, F,
    amps, owner_in, integrals, occ_in, vir_in, out,
    a_all, b_raw, b_hi, b_lo, part, slots, ladder, off_raw, off_hi, off_lo, off_part, off_slots, off_sum,
    own_recv, mate_recv, slot_recv, right_send, left_send, mate_send, slot_send, swap_send, load_sem,
    off_recv, off_send, sum_send, b_send, b_recv,
    owner, occ, vir, small_sem,
):
    r = lax.axis_index("row")
    c = lax.axis_index("col")
    z, co = c // 2, c % 2
    D = amps.shape[0]
    Kr = integrals.shape[0]
    H = Kr - F
    E = Z * R
    rows = 2 * D
    lower = (z < Z // 2).astype(jnp.int32)
    way = 2 * lower - 1
    n_out = jnp.minimum(z, Z - 1 - z)
    at_end = n_out == 0
    beside_end = n_out == 1
    end_z = (1 - lower) * (Z - 1)

    def event(e):
        f = e - 2 * R
        g = f - 2 * R * n_out
        first = e < 2 * R
        paired = f < 2 * R * n_out
        dist = jnp.where(
            first, e // R,
            jnp.where(paired, jnp.where(f % 2 == 0, -(f // (2 * R) + 1), f // (2 * R) + 2), n_out + 2 + g // R),
        )
        j = jnp.where(first, e % R, jnp.where(paired, (f % (2 * R)) // 2, g % R))
        return z + way * dist, flip(r, j, R), dist, j

    def block_copy(zs, rs, width, z_to, c_to, send_sem, recv_sem):
        ref = a_all.at[zs, rs, co, :, pl.ds(0, width)]
        return pltpu.make_async_remote_copy(
            src_ref=ref, dst_ref=ref, send_sem=send_sem, recv_sem=recv_sem.at[zs, rs],
            device_id=(r, z_to * 2 + c_to), device_id_type=MESH,
        )

    def by_width(head_only, fn):
        if F == 0:
            fn(Kr)
            return

        @pl.when(head_only)
        def _():
            fn(H)

        @pl.when(jnp.logical_not(head_only))
        def _():
            fn(Kr)

    def forward(e, act, parts):
        zs, rs, _, _ = event(e)

        def right(width):
            act(block_copy(zs, rs, width, z + 1, co, right_send.at[zs, rs], own_recv))

        def left(width):
            act(block_copy(zs, rs, width, z - 1, co, left_send.at[zs, rs], own_recv))

        def mate(width):
            act(block_copy(zs, rs, width, z, 1 - co, mate_send.at[zs, rs], mate_recv))

        def along(late):
            held = at_end & (zs == z) if F else False

            def when(cond):
                return pl.when(cond & held if late else cond & jnp.logical_not(held))

            @when((zs <= z) & (z < Z - 1))
            def _():
                by_width(z + 1 == Z - 1, right)

            @when((zs >= z) & (z > 0))
            def _():
                by_width(z - 1 == 0, left)

        if parts != "late":
            along(False)
            by_width(at_end & (zs != z), mate)
        if parts != "now" and F:
            along(True)

    def await_block(e, sem, core):
        zs, rs, _, _ = event(e)

        def wait(width):
            ref = a_all.at[zs, rs, core, :, pl.ds(0, width)]
            pltpu.make_async_copy(ref, ref, sem.at[zs, rs]).wait()

        by_width(at_end & (zs != z), wait)

    def product(zs, rs, start, width, hi, lo):
        x = a_all[zs, rs, :, :, start:start + width].reshape(rows, width)
        x_hi, x_lo = split2(x)
        return dot(x_hi, hi) + (dot(x_lo, hi) + dot(x_hi, lo))

    def slot_copy(zs, rs):
        return pltpu.make_async_remote_copy(
            src_ref=part.at[zs, rs], dst_ref=slots.at[zs, r], send_sem=slot_send.at[zs, rs],
            recv_sem=slot_recv.at[zs, r], device_id=(rs, c), device_id_type=MESH,
        )

    def off_copy(zs, rs):
        return pltpu.make_async_remote_copy(
            src_ref=off_part.at[zs, rs], dst_ref=off_slots.at[zs, r], send_sem=off_send.at[zs, rs],
            recv_sem=off_recv.at[zs, r], device_id=(rs, c), device_id_type=MESH,
        )

    def sum_copy(zs):
        return pltpu.make_async_remote_copy(
            src_ref=off_sum.at[zs], dst_ref=slots.at[zs, R], send_sem=sum_send.at[zs],
            recv_sem=slot_recv.at[zs, R], device_id=(r, end_z * 2 + co), device_id_type=MESH,
        )

    def off_product(zs, rs):
        off_part[zs, rs] = product(zs, rs, H, F, off_hi[...], off_lo[...])

        @pl.when(rs != r)
        def _():
            off_copy(zs, rs).start()

    def compute(e):
        zs, rs, dist, j = event(e)
        await_block(e, mate_recv, 1 - co)

        def main(width):
            part[zs, rs] = product(zs, rs, 0, width, b_hi[0:width, :], b_lo[0:width, :])

        by_width(at_end & (zs != z), main)

        @pl.when(rs != r)
        def _():
            slot_copy(zs, rs).start()

        if F:
            @pl.when(beside_end & (dist == -1))
            def _():
                @pl.when(j == 0)
                def _():
                    pltpu.make_async_copy(off_raw, off_raw, b_recv).wait()
                    off_hi[...], off_lo[...] = split2(off_raw[...])

                off_product(z, rs)
                off_product(z + way, rs)

            @pl.when(beside_end & (dist >= 2))
            def _():
                off_product(zs, rs)

    def reduce_off(zs):
        total = off_part[zs, r]
        for k in range(1, R):
            other = flip(r, k, R)
            ref = off_slots.at[zs, other]
            pltpu.make_async_copy(ref, ref, off_recv.at[zs, other]).wait()
            total = total + off_slots[zs, other]
        off_sum[zs] = total
        sum_copy(zs).start()

    def b_tail_copy():
        return pltpu.make_async_remote_copy(
            src_ref=integrals.at[pl.ds(H, F), :], dst_ref=off_raw, send_sem=b_send, recv_sem=b_recv,
            device_id=(r, (end_z + way) * 2 + co), device_id_type=MESH,
        )

    def swap_copy(k):
        other = flip(r, k, R)
        return pltpu.make_async_remote_copy(
            src_ref=amps.at[:, pl.ds(pl.multiple_of(other * Kr, 128), Kr)], dst_ref=a_all.at[z, r, co],
            send_sem=swap_send.at[k], recv_sem=own_recv.at[z, r], device_id=(other, c), device_id_type=MESH,
        )

    mine = pltpu.make_async_copy(
        amps.at[:, pl.ds(pl.multiple_of(r * Kr, 128), Kr)], a_all.at[z, r, co], own_recv.at[z, r]
    )
    mine.start()
    load_b = pltpu.make_async_copy(integrals, b_raw, load_sem)
    load_b.start()
    small = [
        pltpu.make_async_copy(src, dst, small_sem.at[i])
        for i, (src, dst) in enumerate(((owner_in, owner), (occ_in, occ), (vir_in, vir)))
    ]
    for copy in small:
        copy.start()

    barrier = pltpu.get_barrier_semaphore()

    def greet(device):
        pl.semaphore_signal(barrier, inc=1, device_id=device, device_id_type=MESH)

    for k in range(1, R):
        greet((flip(r, k, R), c))
    greet((r, z * 2 + 1 - co))

    @pl.when(z > 0)
    def _():
        greet((r, c - 2))

    @pl.when(z < Z - 1)
    def _():
        greet((r, c + 2))

    pl.semaphore_wait(barrier, R + (z > 0).astype(jnp.int32) + (z < Z - 1).astype(jnp.int32))

    for k in range(1, R):
        swap_copy(k).start()
    if F:
        @pl.when(at_end)
        def _():
            b_tail_copy().start()

    def start(copy):
        copy.start()

    await_block(0, own_recv, co)
    forward(0, start, "now")
    load_b.wait()
    for copy in small:
        copy.wait()
    b_hi[...], b_lo[...] = split2(b_raw[...])

    @pl.loop(1, E)
    def _(e):
        if F:
            late = e - 2 * R
            slot = (2 * late + 2) // 3

            @pl.when(at_end & (late == 0))
            def _():
                b_tail_copy().wait_send()

            @pl.when(at_end & (late >= 0) & (slot < R) & ((3 * slot) // 2 == late))
            def _():
                forward(slot, start, "late")

        await_block(e, own_recv, co)
        forward(e, start, "now")
        compute(e - 1)

    if F:
        @pl.when(beside_end)
        def _():
            reduce_off(z)
            reduce_off(z + way)

    compute(E - 1)
    if F:
        @pl.when(beside_end)
        def _():
            for d in range(2, Z - 1):
                reduce_off(z + way * d)

    def wait_send(copy):
        copy.wait_send()

    for k in range(1, R):
        swap_copy(k).wait_send()
    @pl.loop(0, E)
    def _(e):
        zs, rs, dist, j = event(e)
        forward(e, wait_send, "all")

        @pl.when(rs != r)
        def _():
            slot_copy(zs, rs).wait_send()

        if F:
            @pl.when(beside_end & (dist != -1))
            def _():
                @pl.when(rs != r)
                def _():
                    off_copy(zs, rs).wait_send()

                @pl.when(j == 0)
                def _():
                    sum_copy(zs).wait_send()

    for zs in range(Z):
        total = part[zs, r]
        for k in range(1, R):
            other = flip(r, k, R)
            ref = slots.at[zs, other]
            pltpu.make_async_copy(ref, ref, slot_recv.at[zs, other]).wait()
            total = total + slots[zs, other]
        ladder[zs * rows:(zs + 1) * rows, :] = total
        if F:
            @pl.when(at_end & (z != zs))
            def _(zs=zs):
                ref = slots.at[zs, R]
                pltpu.make_async_copy(ref, ref, slot_recv.at[zs, R]).wait()
                ladder[zs * rows:(zs + 1) * rows, :] += slots[zs, R]

    G = out.shape[0]
    place = (lax.broadcasted_iota(jnp.int32, (G, G), 0) == owner[pl.ds(r, 1), :]).astype(jnp.float32).astype(jnp.bfloat16)
    x = ladder[...]
    h0 = x.astype(jnp.bfloat16)
    x = x - h0.astype(jnp.float32)
    h1, h2 = split2(x)
    placed = (dot(place, h2) + dot(place, h1)) + dot(place, h0)
    diagonal = lax.broadcasted_iota(jnp.int32, (G, G), 0) == lax.broadcasted_iota(jnp.int32, (G, G), 1)
    occ_column = jnp.sum(jnp.where(diagonal, occ[...], 0.0), axis=1, keepdims=True)
    out[...] = placed / (vir[...] - occ_column)


def solution(mesh):
    R, C = mesh.shape["row"], mesh.shape["col"]
    Z = C // 2

    def per_device(amps, row_owner, integrals, occ, vir):
        D = amps.shape[0]
        Kr, N = integrals.shape
        F = Kr * TAIL_PART[0] // TAIL_PART[1] // 128 * 128 if Z >= 4 else 0
        f = max(F, 128)
        G = occ.shape[0]
        rows = 2 * D
        f32, bf16 = jnp.float32, jnp.bfloat16
        dma = pltpu.SemaphoreType.DMA
        vmem = pl.BlockSpec(memory_space=pltpu.VMEM)
        hbm = pl.BlockSpec(memory_space=pl.ANY)
        return pl.pallas_call(
            functools.partial(kernel, R, Z, F),
            out_shape=jax.ShapeDtypeStruct((G, N), f32),
            in_specs=[hbm] * 5,
            out_specs=vmem,
            scratch_shapes=[
                pltpu.VMEM((Z, R, 2, D, Kr), f32),
                pltpu.VMEM((Kr, N), f32),
                pltpu.VMEM((Kr, N), bf16),
                pltpu.VMEM((Kr, N), bf16),
                pltpu.VMEM((Z, R, rows, N), f32),
                pltpu.VMEM((Z, R + 1, rows, N), f32),
                pltpu.VMEM((G, N), f32),
                pltpu.VMEM((f, N), f32),
                pltpu.VMEM((f, N), bf16),
                pltpu.VMEM((f, N), bf16),
                pltpu.VMEM((Z, R, rows, N), f32),
                pltpu.VMEM((Z, R, rows, N), f32),
                pltpu.VMEM((Z, rows, N), f32),
                dma((Z, R)), dma((Z, R)), dma((Z, R + 1)),
                dma((Z, R)), dma((Z, R)), dma((Z, R)), dma((Z, R)), dma((R,)), dma,
                dma((Z, R)), dma((Z, R)), dma((Z,)), dma, dma,
                pltpu.VMEM(row_owner.shape, jnp.int32), pltpu.VMEM((1, G), f32), pltpu.VMEM((1, N), f32), dma((3,)),
            ],
            compiler_params=pltpu.CompilerParams(
                collective_id=0, has_side_effects=True, vmem_limit_bytes=60 * 1024 * 1024
            ),
        )(amps, row_owner, integrals, occ.reshape(1, -1), vir.reshape(1, -1))

    return jax.shard_map(
        per_device,
        mesh=mesh,
        in_specs=(P(("row", "col"), None), P(), P("row", "col"), P("row"), P("col")),
        out_specs=P("row", "col"),
        check_vma=False,
    )
```

```python
import functools

import jax
import jax.numpy as jnp
from jax import lax
from jax.experimental import pallas as pl
from jax.experimental.pallas import tpu as pltpu
from jax.sharding import PartitionSpec as P

MESH = pl.DeviceIdType.MESH
TAIL_PART = (0, 12)


def split2(x):
    hi = x.astype(jnp.bfloat16)
    return hi, (x - hi.astype(jnp.float32)).astype(jnp.bfloat16)


def dot(a, b):
    return jnp.dot(a, b, preferred_element_type=jnp.float32)


def flip(r, j, n):
    out, bit = 0, 1
    while bit < n:
        rb, jb = (r // bit) % 2, (j // bit) % 2
        out = out + bit * (rb + jb - 2 * rb * jb)
        bit *= 2
    return out


def kernel(
    R, Z, F,
    amps, owner_in, integrals, occ_in, vir_in, out,
    a_all, b_raw, b_hi, b_lo, part, slots, ladder, off_raw, off_hi, off_lo, off_part, off_slots, off_sum,
    own_recv, mate_recv, slot_recv, right_send, left_send, mate_send, slot_send, swap_send, load_sem,
    off_recv, off_send, sum_send, b_send, b_recv,
    owner, occ, vir, small_sem,
):
    r = lax.axis_index("row")
    c = lax.axis_index("col")
    z, co = c // 2, c % 2
    D = amps.shape[0]
    Kr = integrals.shape[0]
    H = Kr - F
    E = Z * R
    rows = 2 * D
    lower = (z < Z // 2).astype(jnp.int32)
    way = 2 * lower - 1
    n_out = jnp.minimum(z, Z - 1 - z)
    at_end = n_out == 0
    beside_end = n_out == 1
    end_z = (1 - lower) * (Z - 1)

    def event(e):
        f = e - 2 * R
        g = f - 2 * R * n_out
        first = e < 2 * R
        paired = f < 2 * R * n_out
        dist = jnp.where(
            first, e // R,
            jnp.where(paired, jnp.where(f % 2 == 0, -(f // (2 * R) + 1), f // (2 * R) + 2), n_out + 2 + g // R),
        )
        j = jnp.where(first, e % R, jnp.where(paired, (f % (2 * R)) // 2, g % R))
        turned = jnp.where(first, j, (j + 1) % R)
        return z + way * dist, flip(r, turned, R), dist, j

    def block_copy(zs, rs, width, z_to, c_to, send_sem, recv_sem):
        ref = a_all.at[zs, rs, co, :, pl.ds(0, width)]
        return pltpu.make_async_remote_copy(
            src_ref=ref, dst_ref=ref, send_sem=send_sem, recv_sem=recv_sem.at[zs, rs],
            device_id=(r, z_to * 2 + c_to), device_id_type=MESH,
        )

    def by_width(head_only, fn):
        if F == 0:
            fn(Kr)
            return

        @pl.when(head_only)
        def _():
            fn(H)

        @pl.when(jnp.logical_not(head_only))
        def _():
            fn(Kr)

    def forward(e, act, parts):
        zs, rs, _, _ = event(e)

        def right(width):
            act(block_copy(zs, rs, width, z + 1, co, right_send.at[zs, rs], own_recv))

        def left(width):
            act(block_copy(zs, rs, width, z - 1, co, left_send.at[zs, rs], own_recv))

        def mate(width):
            act(block_copy(zs, rs, width, z, 1 - co, mate_send.at[zs, rs], mate_recv))

        def along(late):
            held = at_end & (zs == z) if F else False

            def when(cond):
                return pl.when(cond & held if late else cond & jnp.logical_not(held))

            @when((zs <= z) & (z < Z - 1))
            def _():
                by_width(z + 1 == Z - 1, right)

            @when((zs >= z) & (z > 0))
            def _():
                by_width(z - 1 == 0, left)

        if parts != "late":
            along(False)
            by_width(at_end & (zs != z), mate)
        if parts != "now" and F:
            along(True)

    def await_block(e, sem, core):
        zs, rs, _, _ = event(e)

        def wait(width):
            ref = a_all.at[zs, rs, core, :, pl.ds(0, width)]
            pltpu.make_async_copy(ref, ref, sem.at[zs, rs]).wait()

        by_width(at_end & (zs != z), wait)

    def product(zs, rs, start, width, hi, lo):
        x = a_all[zs, rs, :, :, start:start + width].reshape(rows, width)
        x_hi, x_lo = split2(x)
        return dot(x_hi, hi) + (dot(x_lo, hi) + dot(x_hi, lo))

    def slot_copy(zs, rs):
        return pltpu.make_async_remote_copy(
            src_ref=part.at[zs, rs], dst_ref=slots.at[zs, r], send_sem=slot_send.at[zs, rs],
            recv_sem=slot_recv.at[zs, r], device_id=(rs, c), device_id_type=MESH,
        )

    def off_copy(zs, rs):
        return pltpu.make_async_remote_copy(
            src_ref=off_part.at[zs, rs], dst_ref=off_slots.at[zs, r], send_sem=off_send.at[zs, rs],
            recv_sem=off_recv.at[zs, r], device_id=(rs, c), device_id_type=MESH,
        )

    def sum_copy(zs):
        return pltpu.make_async_remote_copy(
            src_ref=off_sum.at[zs], dst_ref=slots.at[zs, R], send_sem=sum_send.at[zs],
            recv_sem=slot_recv.at[zs, R], device_id=(r, end_z * 2 + co), device_id_type=MESH,
        )

    def off_product(zs, rs):
        off_part[zs, rs] = product(zs, rs, H, F, off_hi[...], off_lo[...])

        @pl.when(rs != r)
        def _():
            off_copy(zs, rs).start()

    def compute(e):
        zs, rs, dist, j = event(e)
        await_block(e, mate_recv, 1 - co)

        def main(width):
            part[zs, rs] = product(zs, rs, 0, width, b_hi[0:width, :], b_lo[0:width, :])

        by_width(at_end & (zs != z), main)

        @pl.when(rs != r)
        def _():
            slot_copy(zs, rs).start()

        if F:
            @pl.when(beside_end & (dist == -1))
            def _():
                @pl.when(j == 0)
                def _():
                    pltpu.make_async_copy(off_raw, off_raw, b_recv).wait()
                    off_hi[...], off_lo[...] = split2(off_raw[...])

                off_product(z, rs)
                off_product(z + way, rs)

            @pl.when(beside_end & (dist >= 2))
            def _():
                off_product(zs, rs)

    def reduce_off(zs):
        total = off_part[zs, r]
        for k in range(1, R):
            other = flip(r, k, R)
            ref = off_slots.at[zs, other]
            pltpu.make_async_copy(ref, ref, off_recv.at[zs, other]).wait()
            total = total + off_slots[zs, other]
        off_sum[zs] = total
        sum_copy(zs).start()

    def b_tail_copy():
        return pltpu.make_async_remote_copy(
            src_ref=integrals.at[pl.ds(H, F), :], dst_ref=off_raw, send_sem=b_send, recv_sem=b_recv,
            device_id=(r, (end_z + way) * 2 + co), device_id_type=MESH,
        )

    def swap_copy(k):
        other = flip(r, k, R)
        return pltpu.make_async_remote_copy(
            src_ref=amps.at[:, pl.ds(pl.multiple_of(other * Kr, 128), Kr)], dst_ref=a_all.at[z, r, co],
            send_sem=swap_send.at[k], recv_sem=own_recv.at[z, r], device_id=(other, c), device_id_type=MESH,
        )

    mine = pltpu.make_async_copy(
        amps.at[:, pl.ds(pl.multiple_of(r * Kr, 128), Kr)], a_all.at[z, r, co], own_recv.at[z, r]
    )
    mine.start()
    load_b = pltpu.make_async_copy(integrals, b_raw, load_sem)
    load_b.start()
    small = [
        pltpu.make_async_copy(src, dst, small_sem.at[i])
        for i, (src, dst) in enumerate(((owner_in, owner), (occ_in, occ), (vir_in, vir)))
    ]
    for copy in small:
        copy.start()

    barrier = pltpu.get_barrier_semaphore()

    def greet(device):
        pl.semaphore_signal(barrier, inc=1, device_id=device, device_id_type=MESH)

    for k in range(1, R):
        greet((flip(r, k, R), c))
    greet((r, z * 2 + 1 - co))

    @pl.when(z > 0)
    def _():
        greet((r, c - 2))

    @pl.when(z < Z - 1)
    def _():
        greet((r, c + 2))

    pl.semaphore_wait(barrier, R + (z > 0).astype(jnp.int32) + (z < Z - 1).astype(jnp.int32))

    for k in range(1, R):
        swap_copy(k).start()
    if F:
        @pl.when(at_end)
        def _():
            b_tail_copy().start()

    def start(copy):
        copy.start()

    await_block(0, own_recv, co)
    forward(0, start, "now")
    load_b.wait()
    for copy in small:
        copy.wait()
    b_hi[...], b_lo[...] = split2(b_raw[...])

    @pl.loop(1, E)
    def _(e):
        if F:
            late = e - 2 * R
            slot = (2 * late + 2) // 3

            @pl.when(at_end & (late == 0))
            def _():
                b_tail_copy().wait_send()

            @pl.when(at_end & (late >= 0) & (slot < R) & ((3 * slot) // 2 == late))
            def _():
                forward(slot, start, "late")

        await_block(e, own_recv, co)
        forward(e, start, "now")
        compute(e - 1)

    if F:
        @pl.when(beside_end)
        def _():
            reduce_off(z)
            reduce_off(z + way)

    compute(E - 1)
    if F:
        @pl.when(beside_end)
        def _():
            for d in range(2, Z - 1):
                reduce_off(z + way * d)

    def wait_send(copy):
        copy.wait_send()

    for k in range(1, R):
        swap_copy(k).wait_send()
    @pl.loop(0, E)
    def _(e):
        zs, rs, dist, j = event(e)
        forward(e, wait_send, "all")

        @pl.when(rs != r)
        def _():
            slot_copy(zs, rs).wait_send()

        if F:
            @pl.when(beside_end & (dist != -1))
            def _():
                @pl.when(rs != r)
                def _():
                    off_copy(zs, rs).wait_send()

                @pl.when(j == 0)
                def _():
                    sum_copy(zs).wait_send()

    for zs in range(Z):
        total = part[zs, r]
        for k in range(1, R):
            other = flip(r, k, R)
            ref = slots.at[zs, other]
            pltpu.make_async_copy(ref, ref, slot_recv.at[zs, other]).wait()
            total = total + slots[zs, other]
        ladder[zs * rows:(zs + 1) * rows, :] = total
        if F:
            @pl.when(at_end & (z != zs))
            def _(zs=zs):
                ref = slots.at[zs, R]
                pltpu.make_async_copy(ref, ref, slot_recv.at[zs, R]).wait()
                ladder[zs * rows:(zs + 1) * rows, :] += slots[zs, R]

    G = out.shape[0]
    place = (lax.broadcasted_iota(jnp.int32, (G, G), 0) == owner[pl.ds(r, 1), :]).astype(jnp.float32).astype(jnp.bfloat16)
    x = ladder[...]
    h0 = x.astype(jnp.bfloat16)
    x = x - h0.astype(jnp.float32)
    h1, h2 = split2(x)
    placed = (dot(place, h2) + dot(place, h1)) + dot(place, h0)
    diagonal = lax.broadcasted_iota(jnp.int32, (G, G), 0) == lax.broadcasted_iota(jnp.int32, (G, G), 1)
    occ_column = jnp.sum(jnp.where(diagonal, occ[...], 0.0), axis=1, keepdims=True)
    out[...] = placed / (vir[...] - occ_column)


def solution(mesh):
    R, C = mesh.shape["row"], mesh.shape["col"]
    Z = C // 2

    def per_device(amps, row_owner, integrals, occ, vir):
        D = amps.shape[0]
        Kr, N = integrals.shape
        F = Kr * TAIL_PART[0] // TAIL_PART[1] // 128 * 128 if Z >= 4 else 0
        f = max(F, 128)
        G = occ.shape[0]
        rows = 2 * D
        f32, bf16 = jnp.float32, jnp.bfloat16
        dma = pltpu.SemaphoreType.DMA
        vmem = pl.BlockSpec(memory_space=pltpu.VMEM)
        hbm = pl.BlockSpec(memory_space=pl.ANY)
        return pl.pallas_call(
            functools.partial(kernel, R, Z, F),
            out_shape=jax.ShapeDtypeStruct((G, N), f32),
            in_specs=[hbm] * 5,
            out_specs=vmem,
            scratch_shapes=[
                pltpu.VMEM((Z, R, 2, D, Kr), f32),
                pltpu.VMEM((Kr, N), f32),
                pltpu.VMEM((Kr, N), bf16),
                pltpu.VMEM((Kr, N), bf16),
                pltpu.VMEM((Z, R, rows, N), f32),
                pltpu.VMEM((Z, R + 1, rows, N), f32),
                pltpu.VMEM((G, N), f32),
                pltpu.VMEM((f, N), f32),
                pltpu.VMEM((f, N), bf16),
                pltpu.VMEM((f, N), bf16),
                pltpu.VMEM((Z, R, rows, N), f32),
                pltpu.VMEM((Z, R, rows, N), f32),
                pltpu.VMEM((Z, rows, N), f32),
                dma((Z, R)), dma((Z, R)), dma((Z, R + 1)),
                dma((Z, R)), dma((Z, R)), dma((Z, R)), dma((Z, R)), dma((R,)), dma,
                dma((Z, R)), dma((Z, R)), dma((Z,)), dma, dma,
                pltpu.VMEM(row_owner.shape, jnp.int32), pltpu.VMEM((1, G), f32), pltpu.VMEM((1, N), f32), dma((3,)),
            ],
            compiler_params=pltpu.CompilerParams(
                collective_id=0, has_side_effects=True, vmem_limit_bytes=60 * 1024 * 1024
            ),
        )(amps, row_owner, integrals, occ.reshape(1, -1), vir.reshape(1, -1))

    return jax.shard_map(
        per_device,
        mesh=mesh,
        in_specs=(P(("row", "col"), None), P(), P("row", "col"), P("row"), P("col")),
        out_specs=P("row", "col"),
        check_vma=False,
    )
```

```python
import functools

import jax
import jax.numpy as jnp
from jax import lax
from jax.experimental import pallas as pl
from jax.experimental.pallas import tpu as pltpu
from jax.sharding import PartitionSpec as P

MESH = pl.DeviceIdType.MESH
TAIL_PART = (0, 12)


def split2(x):
    hi = x.astype(jnp.bfloat16)
    return hi, (x - hi.astype(jnp.float32)).astype(jnp.bfloat16)


def dot(a, b):
    return jnp.dot(a, b, preferred_element_type=jnp.float32)


def flip(r, j, n):
    out, bit = 0, 1
    while bit < n:
        rb, jb = (r // bit) % 2, (j // bit) % 2
        out = out + bit * (rb + jb - 2 * rb * jb)
        bit *= 2
    return out


def kernel(
    R, Z, F,
    amps, owner_in, integrals, occ_in, vir_in, out,
    a_all, b_raw, b_hi, b_lo, part, slots, ladder, off_raw, off_hi, off_lo, off_part, off_slots, off_sum,
    own_recv, mate_recv, slot_recv, right_send, left_send, mate_send, slot_send, swap_send, load_sem,
    off_recv, off_send, sum_send, b_send, b_recv,
    owner, occ, vir, small_sem,
):
    r = lax.axis_index("row")
    c = lax.axis_index("col")
    z, co = c // 2, c % 2
    D = amps.shape[0]
    Kr = integrals.shape[0]
    H = Kr - F
    E = Z * R
    rows = 2 * D
    lower = (z < Z // 2).astype(jnp.int32)
    way = 2 * lower - 1
    n_out = jnp.minimum(z, Z - 1 - z)
    at_end = n_out == 0
    beside_end = n_out == 1
    end_z = (1 - lower) * (Z - 1)

    def event(e):
        f = e - 2 * R
        g = f - 2 * R * n_out
        first = e < 2 * R
        paired = f < 2 * R * n_out
        dist = jnp.where(
            first, e // R,
            jnp.where(paired, jnp.where(f % 2 == 0, -(f // (2 * R) + 1), f // (2 * R) + 2), n_out + 2 + g // R),
        )
        j = jnp.where(first, e % R, jnp.where(paired, (f % (2 * R)) // 2, g % R))
        turned = jnp.where(first, j, (j + 1) % R)
        return z + way * dist, flip(r, turned, R), dist, j

    def block_copy(zs, rs, width, z_to, c_to, send_sem, recv_sem):
        ref = a_all.at[zs, rs, co, :, pl.ds(0, width)]
        return pltpu.make_async_remote_copy(
            src_ref=ref, dst_ref=ref, send_sem=send_sem, recv_sem=recv_sem.at[zs, rs],
            device_id=(r, z_to * 2 + c_to), device_id_type=MESH,
        )

    def by_width(head_only, fn):
        if F == 0:
            fn(Kr)
            return

        @pl.when(head_only)
        def _():
            fn(H)

        @pl.when(jnp.logical_not(head_only))
        def _():
            fn(Kr)

    def forward(e, act, parts):
        zs, rs, _, _ = event(e)

        def right(width):
            act(block_copy(zs, rs, width, z + 1, co, right_send.at[zs, rs], own_recv))

        def left(width):
            act(block_copy(zs, rs, width, z - 1, co, left_send.at[zs, rs], own_recv))

        def mate(width):
            act(block_copy(zs, rs, width, z, 1 - co, mate_send.at[zs, rs], mate_recv))

        def along(late):
            held = at_end & (zs == z) if F else False

            def when(cond):
                return pl.when(cond & held if late else cond & jnp.logical_not(held))

            @when((zs <= z) & (z < Z - 1))
            def _():
                by_width(z + 1 == Z - 1, right)

            @when((zs >= z) & (z > 0))
            def _():
                by_width(z - 1 == 0, left)

        if parts != "late":
            along(False)
            by_width(at_end & (zs != z), mate)
        if parts != "now" and F:
            along(True)

    def await_block(e, sem, core):
        zs, rs, _, _ = event(e)

        def wait(width):
            ref = a_all.at[zs, rs, core, :, pl.ds(0, width)]
            pltpu.make_async_copy(ref, ref, sem.at[zs, rs]).wait()

        by_width(at_end & (zs != z), wait)

    def product(zs, rs, start, width, hi, lo):
        x = a_all[zs, rs, :, :, start:start + width].reshape(rows, width)
        x_hi, x_lo = split2(x)
        return dot(x_hi, hi) + (dot(x_lo, hi) + dot(x_hi, lo))

    def slot_copy(zs, rs):
        return pltpu.make_async_remote_copy(
            src_ref=part.at[zs, rs], dst_ref=slots.at[zs, r], send_sem=slot_send.at[zs, rs],
            recv_sem=slot_recv.at[zs, r], device_id=(rs, c), device_id_type=MESH,
        )

    def off_copy(zs, rs):
        return pltpu.make_async_remote_copy(
            src_ref=off_part.at[zs, rs], dst_ref=off_slots.at[zs, r], send_sem=off_send.at[zs, rs],
            recv_sem=off_recv.at[zs, r], device_id=(rs, c), device_id_type=MESH,
        )

    def sum_copy(zs):
        return pltpu.make_async_remote_copy(
            src_ref=off_sum.at[zs], dst_ref=slots.at[zs, R], send_sem=sum_send.at[zs],
            recv_sem=slot_recv.at[zs, R], device_id=(r, end_z * 2 + co), device_id_type=MESH,
        )

    def off_product(zs, rs):
        off_part[zs, rs] = product(zs, rs, H, F, off_hi[...], off_lo[...])

        @pl.when(rs != r)
        def _():
            off_copy(zs, rs).start()

    def compute(e):
        zs, rs, dist, j = event(e)
        await_block(e, mate_recv, 1 - co)

        def main(width):
            part[zs, rs] = product(zs, rs, 0, width, b_hi[0:width, :], b_lo[0:width, :])

        by_width(at_end & (zs != z), main)

        @pl.when(rs != r)
        def _():
            slot_copy(zs, rs).start()

        if F:
            @pl.when(beside_end & (dist == -1))
            def _():
                @pl.when(j == 0)
                def _():
                    pltpu.make_async_copy(off_raw, off_raw, b_recv).wait()
                    off_hi[...], off_lo[...] = split2(off_raw[...])

                off_product(z, rs)
                off_product(z + way, rs)

            @pl.when(beside_end & (dist >= 2))
            def _():
                off_product(zs, rs)

    def reduce_off(zs):
        total = off_part[zs, r]
        for k in range(1, R):
            other = flip(r, k, R)
            ref = off_slots.at[zs, other]
            pltpu.make_async_copy(ref, ref, off_recv.at[zs, other]).wait()
            total = total + off_slots[zs, other]
        off_sum[zs] = total
        sum_copy(zs).start()

    def b_tail_copy():
        return pltpu.make_async_remote_copy(
            src_ref=integrals.at[pl.ds(H, F), :], dst_ref=off_raw, send_sem=b_send, recv_sem=b_recv,
            device_id=(r, (end_z + way) * 2 + co), device_id_type=MESH,
        )

    def swap_copy(k):
        other = flip(r, k, R)
        return pltpu.make_async_remote_copy(
            src_ref=amps.at[:, pl.ds(pl.multiple_of(other * Kr, 128), Kr)], dst_ref=a_all.at[z, r, co],
            send_sem=swap_send.at[k], recv_sem=own_recv.at[z, r], device_id=(other, c), device_id_type=MESH,
        )

    mine = pltpu.make_async_copy(
        amps.at[:, pl.ds(pl.multiple_of(r * Kr, 128), Kr)], a_all.at[z, r, co], own_recv.at[z, r]
    )
    mine.start()
    load_b = pltpu.make_async_copy(integrals, b_raw, load_sem)
    load_b.start()
    small = [
        pltpu.make_async_copy(src, dst, small_sem.at[i])
        for i, (src, dst) in enumerate(((owner_in, owner), (occ_in, occ), (vir_in, vir)))
    ]
    for copy in small:
        copy.start()

    barrier = pltpu.get_barrier_semaphore()

    def greet(device):
        pl.semaphore_signal(barrier, inc=1, device_id=device, device_id_type=MESH)

    for k in range(1, R):
        greet((flip(r, k, R), c))
    greet((r, z * 2 + 1 - co))

    @pl.when(z > 0)
    def _():
        greet((r, c - 2))

    @pl.when(z < Z - 1)
    def _():
        greet((r, c + 2))

    pl.semaphore_wait(barrier, R + (z > 0).astype(jnp.int32) + (z < Z - 1).astype(jnp.int32))

    for k in range(1, R):
        swap_copy(k).start()
    if F:
        @pl.when(at_end)
        def _():
            b_tail_copy().start()

    def start(copy):
        copy.start()

    await_block(0, own_recv, co)
    forward(0, start, "now")
    load_b.wait()
    for copy in small:
        copy.wait()
    b_hi[...], b_lo[...] = split2(b_raw[...])

    @pl.loop(1, E)
    def _(e):
        if F:
            late = e - 2 * R
            slot = (2 * late + 2) // 3

            @pl.when(at_end & (late == 0))
            def _():
                b_tail_copy().wait_send()

            @pl.when(at_end & (late >= 0) & (slot < R) & ((3 * slot) // 2 == late))
            def _():
                forward(slot, start, "late")

        early = at_end & (e > E - R)

        @pl.when(early)
        def _():
            compute(e - 1)

        await_block(e, own_recv, co)
        forward(e, start, "now")

        @pl.when(jnp.logical_not(early))
        def _():
            compute(e - 1)

    if F:
        @pl.when(beside_end)
        def _():
            reduce_off(z)
            reduce_off(z + way)

    compute(E - 1)
    if F:
        @pl.when(beside_end)
        def _():
            for d in range(2, Z - 1):
                reduce_off(z + way * d)

    def wait_send(copy):
        copy.wait_send()

    for k in range(1, R):
        swap_copy(k).wait_send()
    @pl.loop(0, E)
    def _(e):
        zs, rs, dist, j = event(e)
        forward(e, wait_send, "all")

        @pl.when(rs != r)
        def _():
            slot_copy(zs, rs).wait_send()

        if F:
            @pl.when(beside_end & (dist != -1))
            def _():
                @pl.when(rs != r)
                def _():
                    off_copy(zs, rs).wait_send()

                @pl.when(j == 0)
                def _():
                    sum_copy(zs).wait_send()

    for zs in range(Z):
        total = part[zs, r]
        for k in range(1, R):
            other = flip(r, k, R)
            ref = slots.at[zs, other]
            pltpu.make_async_copy(ref, ref, slot_recv.at[zs, other]).wait()
            total = total + slots[zs, other]
        ladder[zs * rows:(zs + 1) * rows, :] = total
        if F:
            @pl.when(at_end & (z != zs))
            def _(zs=zs):
                ref = slots.at[zs, R]
                pltpu.make_async_copy(ref, ref, slot_recv.at[zs, R]).wait()
                ladder[zs * rows:(zs + 1) * rows, :] += slots[zs, R]

    G = out.shape[0]
    place = (lax.broadcasted_iota(jnp.int32, (G, G), 0) == owner[pl.ds(r, 1), :]).astype(jnp.float32).astype(jnp.bfloat16)
    x = ladder[...]
    h0 = x.astype(jnp.bfloat16)
    x = x - h0.astype(jnp.float32)
    h1, h2 = split2(x)
    placed = (dot(place, h2) + dot(place, h1)) + dot(place, h0)
    diagonal = lax.broadcasted_iota(jnp.int32, (G, G), 0) == lax.broadcasted_iota(jnp.int32, (G, G), 1)
    occ_column = jnp.sum(jnp.where(diagonal, occ[...], 0.0), axis=1, keepdims=True)
    out[...] = placed / (vir[...] - occ_column)


def solution(mesh):
    R, C = mesh.shape["row"], mesh.shape["col"]
    Z = C // 2

    def per_device(amps, row_owner, integrals, occ, vir):
        D = amps.shape[0]
        Kr, N = integrals.shape
        F = Kr * TAIL_PART[0] // TAIL_PART[1] // 128 * 128 if Z >= 4 else 0
        f = max(F, 128)
        G = occ.shape[0]
        rows = 2 * D
        f32, bf16 = jnp.float32, jnp.bfloat16
        dma = pltpu.SemaphoreType.DMA
        vmem = pl.BlockSpec(memory_space=pltpu.VMEM)
        hbm = pl.BlockSpec(memory_space=pl.ANY)
        return pl.pallas_call(
            functools.partial(kernel, R, Z, F),
            out_shape=jax.ShapeDtypeStruct((G, N), f32),
            in_specs=[hbm] * 5,
            out_specs=vmem,
            scratch_shapes=[
                pltpu.VMEM((Z, R, 2, D, Kr), f32),
                pltpu.VMEM((Kr, N), f32),
                pltpu.VMEM((Kr, N), bf16),
                pltpu.VMEM((Kr, N), bf16),
                pltpu.VMEM((Z, R, rows, N), f32),
                pltpu.VMEM((Z, R + 1, rows, N), f32),
                pltpu.VMEM((G, N), f32),
                pltpu.VMEM((f, N), f32),
                pltpu.VMEM((f, N), bf16),
                pltpu.VMEM((f, N), bf16),
                pltpu.VMEM((Z, R, rows, N), f32),
                pltpu.VMEM((Z, R, rows, N), f32),
                pltpu.VMEM((Z, rows, N), f32),
                dma((Z, R)), dma((Z, R)), dma((Z, R + 1)),
                dma((Z, R)), dma((Z, R)), dma((Z, R)), dma((Z, R)), dma((R,)), dma,
                dma((Z, R)), dma((Z, R)), dma((Z,)), dma, dma,
                pltpu.VMEM(row_owner.shape, jnp.int32), pltpu.VMEM((1, G), f32), pltpu.VMEM((1, N), f32), dma((3,)),
            ],
            compiler_params=pltpu.CompilerParams(
                collective_id=0, has_side_effects=True, vmem_limit_bytes=60 * 1024 * 1024
            ),
        )(amps, row_owner, integrals, occ.reshape(1, -1), vir.reshape(1, -1))

    return jax.shard_map(
        per_device,
        mesh=mesh,
        in_specs=(P(("row", "col"), None), P(), P("row", "col"), P("row"), P("col")),
        out_specs=P("row", "col"),
        check_vma=False,
    )
```
